256 devices in a mesh: row: 64 (over z_hi, x, y, core), col: 4 (over z_lo).
Axes of the slice: x: 4, y: 4, z: 8 (z_hi: 2, z_lo: 4; z = z_hi * 4 + z_lo), core: 2. Of those that a mesh axis runs over, the one named last changes fastest.
Arguments:
- tokens: bfloat16 [1024, 8192], P('row', 'col'), may hold values from -6 to 6
- out_grad: bfloat16 [1024, 8192], P('row', 'col'), may hold values from -6 to 6
- gate_weight: bfloat16 [8192, 16384], P('col', 'row'), may hold values from -0.0625 to 0.0625
- up_weight: bfloat16 [8192, 16384], P('col', 'row'), may hold values from -0.0625 to 0.0625
- down_weight: bfloat16 [16384, 8192], P('row', 'col'), may hold values from -0.046875 to 0.046875
- gate_mask: int32 [64, 128], P('col', 'row'), may hold values 0 or 1
- up_mask: int32 [64, 128], P('col', 'row'), may hold values 0 or 1
- down_mask: int32 [128, 64], P('row', 'col'), may hold values 0 or 1
Outputs:
- input_grad: float32 [1024, 8192], P('row', 'col')
- gate_grad: float32 [8192, 16384], P('col', 'row')
- up_grad: float32 [8192, 16384], P('col', 'row')
- down_grad: float32 [16384, 8192], P('row', 'col')
The draws below stay inside these ranges and needn't reach their ends.
All inputs are finite; a program needn't handle non-finite values. No bound on the sum of `gate_mask` or of `up_mask` or of `down_mask` on one device may be relied on, other than what follows from the above.
Results may differ from the reference program's by a relative error of at most 0.0029.
Values may be sent and summed in bfloat16 or wider, within the bound.
No kernel may reach another device: no remote copies, remote signals or barrier semaphores. Data moves between devices by JAX's collectives and lax.ppermute only.
A program may use at most 128 MiB of HBM per device.

```python
import jax
import jax.numpy as jnp
from jax import lax

D = 8192
FF = 16384
BLOCK = 128
TOKENS = 1024


def plant(array, own_key, smallest, high):
    dims = array.shape
    index_at = [jax.random.randint(jax.random.fold_in(own_key, axis), (), 0, dims[axis]) for axis in range(len(dims))]
    array = array.at[tuple(index_at)].set(smallest)
    longest = dims.index(max(dims))
    index_at[longest] = (index_at[longest] + 1) % dims[longest]
    return array.at[tuple(index_at)].set(high)


def block_scale(own_key, extent, pieces, smallest, high):
    loudness, own = 1.0, jax.random.fold_in(own_key, 6)
    for position, parts in pieces:
        steps = jnp.exp(jax.random.uniform(jax.random.fold_in(own, position), (parts,), jnp.float32, smallest / len(pieces), high / len(pieces)))
        loudness = loudness * jnp.repeat(steps, extent[position] // parts).reshape([-1 if axis == position else 1 for axis in range(len(extent))])
    return loudness


def bell_draw(own_key, extent, deviation, limit, pieces=(), dtype=jnp.bfloat16):
    drawn = deviation * jax.random.normal(own_key, extent, jnp.float32)
    if pieces:
        drawn = drawn * block_scale(own_key, extent, pieces, -0.22, 0.18)
    return jnp.clip(drawn, -limit, limit).astype(dtype)


def setup_inputs(seed: int = 0) -> dict:
    seeds = jax.random.split(jax.random.key(seed), 9)
    tokens = bell_draw(seeds[0], (TOKENS, D), 1.0, 6.0, ((0, 64), (1, 4)))
    out_grad = bell_draw(seeds[1], (TOKENS, D), 1.0, 6.0, ((0, 64), (1, 4)))
    gate_weight = bell_draw(seeds[2], (D, FF), D ** -0.5, 0.0625, ((0, 4), (1, 64)))
    up_weight = bell_draw(seeds[3], (D, FF), D ** -0.5, 0.0625, ((0, 4), (1, 64)))
    down_weight = bell_draw(seeds[4], (FF, D), FF ** -0.5, 0.046875, ((0, 64), (1, 4)))
    gate_mask = plant((jax.random.randint(seeds[5], (D // BLOCK, FF // BLOCK), 0, 2) < 1).astype(jnp.int32), jax.random.fold_in(seeds[5], 1), 0, 1)
    up_mask = plant((jax.random.randint(seeds[6], (D // BLOCK, FF // BLOCK), 0, 2) < 1).astype(jnp.int32), jax.random.fold_in(seeds[6], 1), 0, 1)
    down_mask = plant((jax.random.randint(seeds[7], (FF // BLOCK, D // BLOCK), 0, 2) < 1).astype(jnp.int32), jax.random.fold_in(seeds[7], 1), 0, 1)
    return dict(tokens=tokens, out_grad=out_grad, gate_weight=gate_weight, up_weight=up_weight, down_weight=down_weight, gate_mask=gate_mask, up_mask=up_mask, down_mask=down_mask)


def expand(mask, rows, cols):
    wide = jnp.broadcast_to(mask[:, None, :, None], (rows, BLOCK, cols, BLOCK))
    return wide.reshape(rows * BLOCK, cols * BLOCK).astype(jnp.bfloat16)


def reference(tokens, out_grad, gate_weight, up_weight, down_weight, gate_mask, up_mask, down_mask):
    gate_eff = gate_weight * expand(gate_mask, gate_mask.shape[0], gate_mask.shape[1])
    up_eff = up_weight * expand(up_mask, up_mask.shape[0], up_mask.shape[1])
    down_eff = down_weight * expand(down_mask, down_mask.shape[0], down_mask.shape[1])
    gate = jnp.dot(tokens, gate_eff, preferred_element_type=jnp.float32)
    up = jnp.dot(tokens, up_eff, preferred_element_type=jnp.float32)
    hidden_grad = lax.dot_general(out_grad, down_eff, (((1,), (1,)), ((), ())), preferred_element_type=jnp.float32)
    sig = jax.nn.sigmoid(gate)
    swish = gate * sig
    hidden = (swish * up).astype(jnp.bfloat16)
    gate_delta = (hidden_grad * up * sig * (1.0 + gate * (1.0 - sig))).astype(jnp.bfloat16)
    up_delta = (hidden_grad * swish).astype(jnp.bfloat16)
    input_grad = lax.dot_general(gate_delta, gate_eff, (((1,), (1,)), ((), ())), preferred_element_type=jnp.float32)
    input_grad = input_grad + lax.dot_general(up_delta, up_eff, (((1,), (1,)), ((), ())), preferred_element_type=jnp.float32)
    contract = (((0,), (0,)), ((), ()))
    gate_grad = lax.dot_general(tokens, gate_delta, contract, preferred_element_type=jnp.float32) * expand(gate_mask, gate_mask.shape[0], gate_mask.shape[1]).astype(jnp.float32)
    up_grad = lax.dot_general(tokens, up_delta, contract, preferred_element_type=jnp.float32) * expand(up_mask, up_mask.shape[0], up_mask.shape[1]).astype(jnp.float32)
    down_grad = lax.dot_general(hidden, out_grad, contract, preferred_element_type=jnp.float32) * expand(down_mask, down_mask.shape[0], down_mask.shape[1]).astype(jnp.float32)
    return input_grad, gate_grad, up_grad, down_grad
```

```python
import jax
import jax.numpy as jnp
from jax import lax
from jax.sharding import PartitionSpec as P

BLOCK = 128
ZH, X, Y, CORE = 2, 4, 4, 2
COL = 4
TRANSPOSED = (((1,), (1,)), ((), ()))
CONTRACT = (((0,), (0,)), ((), ()))
TOP = 14.0


def row_pairs(move):
    pairs = []
    for zh in range(ZH):
        for x in range(X):
            for y in range(Y):
                for core in range(CORE):
                    a, b, c, d = move(zh, x, y, core)
                    target = (((a % ZH) * X + b % X) * Y + c % Y) * CORE + d % CORE
                    pairs.append((((zh * X + x) * Y + y) * CORE + core, target))
    return pairs


def send_zh(v):
    return lax.ppermute(v, "row", row_pairs(lambda zh, x, y, core: (zh + 1, x, y, core)))


def send_x(v, by):
    return lax.ppermute(v, "row", row_pairs(lambda zh, x, y, core: (zh, x + by, y, core)))


def send_y(v, by):
    return lax.ppermute(v, "row", row_pairs(lambda zh, x, y, core: (zh, x, y + by, core)))


def send_core(v):
    return lax.ppermute(v, "row", row_pairs(lambda zh, x, y, core: (zh, x, y, core + 1)))


def send_col(v, by):
    return lax.ppermute(v, "col", [(i, (i + by) % COL) for i in range(COL)])


def expand(mask):
    rows = mask.shape[0]
    cols = mask.shape[1]
    wide = jnp.broadcast_to(mask[:, None, :, None], (rows, BLOCK, cols, BLOCK))
    return wide.reshape(rows * BLOCK, cols * BLOCK).astype(jnp.bfloat16)


def gather_plane(v):
    v = jnp.concatenate([v] + [send_y(v, d) for d in (1, 2, 3)], axis=1)
    return jnp.concatenate([v] + [send_x(v, d) for d in (1, 2, 3)], axis=1)


def sum_over_col(part):
    me = lax.axis_index("col")
    tokens, width = part.shape
    rows = tokens // COL
    largest = jnp.max(jnp.abs(part), axis=0, keepdims=True)
    power = jnp.clip(jnp.ceil(jnp.log2(largest)), -100.0, 100.0)
    coded = (part * jnp.exp2(TOP - power)).astype(jnp.float16)
    tail = jnp.broadcast_to(power, (16, width)).astype(jnp.float16)
    total = lax.dynamic_slice_in_dim(part, me * rows, rows, 0)
    for d in (1, 2, 3):
        block = lax.dynamic_slice_in_dim(coded, lax.rem(me + d, COL) * rows, rows, 0)
        got = send_col(jnp.concatenate([block, tail], axis=0), d).astype(jnp.float32)
        total = total + got[:rows] * jnp.exp2(got[rows : rows + 1] - TOP)
    return total


def gather_over_col(v):
    me = lax.axis_index("col")
    rows, width = v.shape
    every = jnp.zeros((COL * rows, width), v.dtype)
    every = lax.dynamic_update_slice_in_dim(every, v, me * rows, 0)
    for d in (1, 2, 3):
        got = send_col(v, d)
        every = lax.dynamic_update_slice_in_dim(every, got, lax.rem(me + COL - d, COL) * rows, 0)
    return every


def sum_over_row(other, own):
    total = own + send_core(other)
    for send, count in ((send_x, X), (send_y, Y)):
        rows = total.shape[0] // count
        kept = total[:rows]
        for d in range(1, count):
            kept = kept + send(total[d * rows : (d + 1) * rows].astype(jnp.bfloat16), -d).astype(jnp.float32)
        total = kept
    return total


def per_device(
    tokens, out_grad, gate_weight, up_weight, down_weight, gate_mask, up_mask, down_mask
):
    width = gate_weight.shape[1]
    gate_keep = expand(gate_mask)
    up_keep = expand(up_mask)
    down_keep = expand(down_mask)
    both_eff = jnp.concatenate([gate_weight * gate_keep, up_weight * up_keep], axis=1)
    down_eff = down_weight * down_keep

    first = jnp.stack([tokens, out_grad])
    second = send_zh(first)
    outs = []
    for mine in (first, second):
        own_v = gather_plane(mine)
        other_v = send_core(own_v)
        parts = []
        for v in (own_v, other_v):
            parts.append(
                jnp.concatenate(
                    [
                        jnp.dot(v[0], both_eff, preferred_element_type=jnp.float32),
                        lax.dot_general(v[1], down_eff, TRANSPOSED, preferred_element_type=jnp.float32),
                    ],
                    axis=1,
                )
            )
        summed = sum_over_col(jnp.concatenate(parts, axis=0))
        gate = summed[:, :width]
        up_val = summed[:, width : 2 * width]
        hidden_grad = summed[:, 2 * width :]
        sig = jax.nn.sigmoid(gate)
        swish = gate * sig
        hidden = (swish * up_val).astype(jnp.bfloat16)
        gate_delta = (hidden_grad * up_val * sig * (1.0 + gate * (1.0 - sig))).astype(jnp.bfloat16)
        up_delta = (hidden_grad * swish).astype(jnp.bfloat16)
        every = gather_over_col(jnp.concatenate([hidden, gate_delta, up_delta], axis=1))
        deltas = every[:, width:]
        half = deltas.shape[0] // 2
        own = lax.dot_general(deltas[:half], both_eff, TRANSPOSED, preferred_element_type=jnp.float32)
        other = lax.dot_general(deltas[half:], both_eff, TRANSPOSED, preferred_element_type=jnp.float32)
        total = sum_over_row(other, own)
        xs = jnp.concatenate([own_v[0], other_v[0]], axis=0)
        dys = jnp.concatenate([own_v[1], other_v[1]], axis=0)
        outs.append(
            (
                total,
                lax.dot_general(xs, every[:, width : 2 * width], CONTRACT, preferred_element_type=jnp.float32),
                lax.dot_general(xs, every[:, 2 * width :], CONTRACT, preferred_element_type=jnp.float32),
                lax.dot_general(every[:, :width], dys, CONTRACT, preferred_element_type=jnp.float32),
            )
        )
    a, b = outs
    return (
        a[0] + send_zh(b[0]),
        (a[1] + b[1]) * gate_keep.astype(jnp.float32),
        (a[2] + b[2]) * up_keep.astype(jnp.float32),
        (a[3] + b[3]) * down_keep.astype(jnp.float32),
    )


def solution(mesh):
    return jax.shard_map(
        per_device,
        mesh=mesh,
        in_specs=(
            P("row", "col"),
            P("row", "col"),
            P("col", "row"),
            P("col", "row"),
            P("row", "col"),
            P("col", "row"),
            P("col", "row"),
            P("row", "col"),
        ),
        out_specs=(P("row", "col"), P("col", "row"), P("col", "row"), P("row", "col")),
        check_vma=False,
    )
```

```python
import jax
import jax.numpy as jnp
from jax import lax
from jax.experimental import pallas as pl
from jax.experimental.pallas import tpu as pltpu
from jax.sharding import PartitionSpec as P

BLOCK = 128
ZH, X, Y, CORE = 2, 4, 4, 2
COL = 4
TRANSPOSED = (((1,), (1,)), ((), ()))
CONTRACT = (((0,), (0,)), ((), ()))


def row_of(zh, x, y, core):
    return ((zh * X + x) * Y + y) * CORE + core


PLACES = [(zh, x, y, core) for zh in range(ZH) for x in range(X) for y in range(Y) for core in range(CORE)]
def send_zh(v):
    return lax.ppermute(v, "row", [(row_of(*p), row_of(1 - p[0], *p[1:])) for p in PLACES])


def send_core(v):
    return lax.ppermute(v, "row", [(row_of(*p), row_of(*p[:3], 1 - p[3])) for p in PLACES])


def step(place, along_x, by):
    zh, x, y, core = place
    return row_of(zh, (x + by) % X, y, core) if along_x else row_of(zh, x, (y + by) % Y, core)


def send_small(v, by):
    return lax.ppermute(v, "row", [(row_of(*p), step(p, p[3] == 1, by)) for p in PLACES])


def send_big(v, by):
    return lax.ppermute(v, "row", [(row_of(*p), step(p, p[3] == 0, by)) for p in PLACES])


def send_col(v, by):
    return lax.ppermute(v, "col", [(i, (i + by) % COL) for i in range(COL)])


def gather_over_col(v):
    me = lax.axis_index("col")
    rows = v.shape[0]
    got = [send_col(v, d) for d in (1, 2, 3)]
    every = lax.dynamic_update_slice_in_dim(jnp.zeros((COL * rows, v.shape[1]), v.dtype), v, me * rows, 0)
    for d, block in zip((1, 2, 3), got):
        every = lax.dynamic_update_slice_in_dim(every, block, lax.rem(me + COL - d, COL) * rows, 0)
    return every


def sum_along(blocks, send):
    kept = blocks[0]
    for d in (1, 2, 3):
        kept = kept + send(blocks[d].astype(jnp.bfloat16), -d).astype(jnp.float32)
    return kept


def after(v, *earlier):
    return lax.optimization_barrier((v,) + earlier)[0]


def expand(mask):
    rows = mask.shape[0]
    cols = mask.shape[1]
    wide = jnp.broadcast_to(mask[:, None, :, None], (rows, BLOCK, cols, BLOCK))
    return wide.reshape(rows * BLOCK, cols * BLOCK).astype(jnp.bfloat16)


def prune_kernel(gate_mask, up_mask, down_mask, gate, up, down, both_eff, down_eff):
    width = gate.shape[1]
    for mask, source, target, offset in (
        (gate_mask, gate, both_eff, 0),
        (up_mask, up, both_eff, width),
        (down_mask, down, down_eff, 0),
    ):
        for i in range(mask.shape[0]):
            for j in range(mask.shape[1]):
                rows = slice(i * BLOCK, (i + 1) * BLOCK)
                block = source[rows, j * BLOCK : (j + 1) * BLOCK]
                target[rows, offset + j * BLOCK : offset + (j + 1) * BLOCK] = jnp.where(
                    mask[i, j] != 0, block, jnp.zeros_like(block)
                )


def prune(gate_mask, up_mask, down_mask, gate, up, down):
    depth, width = gate.shape
    scalars = pl.BlockSpec(memory_space=pltpu.SMEM)
    whole = pl.BlockSpec(memory_space=pltpu.VMEM)
    return pl.pallas_call(
        prune_kernel,
        in_specs=[scalars] * 3 + [whole] * 3,
        out_specs=[whole] * 2,
        out_shape=[
            jax.ShapeDtypeStruct((depth, 2 * width), jnp.bfloat16),
            jax.ShapeDtypeStruct((width, depth), jnp.bfloat16),
        ],
        compiler_params=pltpu.CompilerParams(vmem_limit_bytes=32 * 1024 * 1024),
    )(gate_mask, up_mask, down_mask, gate, up, down)


def code(part):
    largest = jnp.max(jnp.abs(part), axis=0, keepdims=True)
    power = jnp.clip(jnp.ceil(jnp.log2(largest)), -100.0, 100.0)
    return (part * jnp.exp2(14.0 - power)).astype(jnp.float16), jnp.broadcast_to(power, (8, part.shape[1])).astype(jnp.float16)


def sends_over_col(part, *earlier):
    me = lax.axis_index("col")
    rows = part.shape[0] // COL
    coded, powers = code(part)
    kept = lax.dynamic_slice_in_dim(part, me * rows, rows, 0)
    sent = [
        jnp.concatenate([lax.dynamic_slice_in_dim(coded, lax.rem(me + d, COL) * rows, rows, 0), powers], axis=0)
        for d in (1, 2, 3)
    ]
    sent = lax.optimization_barrier((*sent, *earlier))[:3]
    return [kept] + [send_col(v, d) for v, d in zip(sent, (1, 2, 3))]


def sum_over_col(blocks):
    total = blocks[0]
    rows = total.shape[0]
    for v in blocks[1:]:
        got = v.astype(jnp.float32)
        total = total + got[:rows] * jnp.exp2(got[rows : rows + 1] - 14.0)
    return total


def swiglu_grads(summed, width):
    hiddens, deltas = [], []
    for core in (0, 1):
        gate = summed[:, 2 * core * width : (2 * core + 1) * width]
        up_val = summed[:, (2 * core + 1) * width : (2 * core + 2) * width]
        hidden_grad = summed[:, (4 + core) * width : (5 + core) * width]
        sig = jax.nn.sigmoid(gate)
        swish = gate * sig
        hiddens.append((swish * up_val).astype(jnp.bfloat16))
        deltas.append((hidden_grad * up_val * sig * (1.0 + gate * (1.0 - sig))).astype(jnp.bfloat16))
        deltas.append((hidden_grad * swish).astype(jnp.bfloat16))
    return jnp.concatenate(hiddens, axis=1), jnp.concatenate(deltas, axis=1)


def per_device(
    tokens, out_grad, gate_weight, up_weight, down_weight, gate_mask, up_mask, down_mask
):
    depth, width = gate_weight.shape
    first = jnp.stack([tokens, out_grad])
    second = send_zh(first)

    masks = lax.optimization_barrier((gate_mask, up_mask, down_mask, second))[:3]
    both_eff, down_eff = prune(*masks, gate_weight, up_weight, down_weight)
    both_eff = both_eff, send_core(both_eff)
    down_eff = down_eff, send_core(down_eff)

    v = jnp.concatenate([first, second], axis=1)
    v = jnp.concatenate([v] + [send_small(v, d) for d in (1, 2, 3)], axis=1)
    def forward(own, *earlier):
        parts = [jnp.dot(own[0], w, preferred_element_type=jnp.float32) for w in both_eff]
        parts += [lax.dot_general(own[1], w, TRANSPOSED, preferred_element_type=jnp.float32) for w in down_eff]
        return sends_over_col(jnp.concatenate(parts, axis=1), *earlier)

    def backward(every):
        return sum(
            lax.dot_general(
                every[:, 2 * i * width : 2 * (i + 1) * width], w, TRANSPOSED, preferred_element_type=jnp.float32
            )
            for i, w in enumerate(both_eff)
        )

    blocks_a = forward(v)
    got = [send_big(v, d) for d in (1, 2, 3)]
    hidden_a, deltas_a = swiglu_grads(sum_over_col(blocks_a), width)
    *got, deltas_a = lax.optimization_barrier((*got, deltas_a))
    own_b = jnp.concatenate(got, axis=1)
    every_a = gather_over_col(deltas_a)
    hidden_b, deltas_b = swiglu_grads(sum_over_col(forward(own_b, every_a)), width)
    other_a, other_b = send_core(v), send_core(own_b)
    deltas_b = lax.optimization_barrier((deltas_b, other_a, other_b))[0]
    every_b = gather_over_col(deltas_b)
    total_a, total_b = backward(every_a), backward(every_b)
    blocks = jnp.split(total_b.astype(jnp.bfloat16), 3, axis=0)
    came = [send_big(v, -d) for v, d in zip(blocks, (1, 2, 3))]
    every = jnp.concatenate([every_a, every_b], axis=0)
    swapped = send_core(every[:, 2 * width :])
    hidden_a, hidden_b = lax.optimization_barrier((hidden_a, hidden_b, swapped))[:2]
    hidden = gather_over_col(jnp.concatenate([hidden_a, hidden_b], axis=0)).reshape(COL, -1, 2 * width)
    cut = hidden_a.shape[0]
    hidden = jnp.concatenate([hidden[:, :cut].reshape(-1, 2 * width), hidden[:, cut:].reshape(-1, 2 * width)], axis=0)
    hidden_other = send_core(hidden[:, width:])
    own = jnp.concatenate([v, own_b], axis=1)
    other = jnp.concatenate([other_a, other_b], axis=1)
    masks = lax.optimization_barrier((gate_mask, up_mask, down_mask, deltas_b))[:3]
    gate_keep, up_keep, down_keep = (expand(mask) for mask in masks)

    def contract(a, b):
        return lax.dot_general(a, b, CONTRACT, preferred_element_type=jnp.float32)

    gate_grad = contract(own[0], every[:, :width]) + contract(other[0], swapped[:, :width])
    up_grad = contract(own[0], every[:, width : 2 * width]) + contract(other[0], swapped[:, width:])
    gate_grad = gate_grad * gate_keep.astype(jnp.float32)
    up_grad = up_grad * up_keep.astype(jnp.float32)
    total = total_a + came[0].astype(jnp.float32) + came[1].astype(jnp.float32) + came[2].astype(jnp.float32)
    total, gate_grad, up_grad = lax.optimization_barrier((total, gate_grad, up_grad))
    rows = total.shape[0] // 4
    total = sum_along([total[d * rows : (d + 1) * rows] for d in range(4)], send_small)
    rows = rows // 2
    total = total[:rows] + send_zh(total[rows:])
    down_grad = contract(hidden[:, :width], own[1]) + contract(hidden_other, other[1])
    down_grad = down_grad * down_keep.astype(jnp.float32)
    return total, gate_grad, up_grad, down_grad


def solution(mesh):
    return jax.shard_map(
        per_device,
        mesh=mesh,
        in_specs=(
            P("row", "col"),
            P("row", "col"),
            P("col", "row"),
            P("col", "row"),
            P("row", "col"),
            P("col", "row"),
            P("col", "row"),
            P("row", "col"),
        ),
        out_specs=(P("row", "col"), P("col", "row"), P("col", "row"), P("row", "col")),
        check_vma=False,
    )
```

```python
import jax
import jax.numpy as jnp
from jax import lax
from jax.experimental import pallas as pl
from jax.experimental.pallas import tpu as pltpu
from jax.sharding import PartitionSpec as P

BLOCK = 128
ZH, X, Y, CORE = 2, 4, 4, 2
COL = 4
TRANSPOSED = (((1,), (1,)), ((), ()))
CONTRACT = (((0,), (0,)), ((), ()))


def row_of(zh, x, y, core):
    return ((zh * X + x) * Y + y) * CORE + core


PLACES = [(zh, x, y, core) for zh in range(ZH) for x in range(X) for y in range(Y) for core in range(CORE)]
def send_zh(v):
    return lax.ppermute(v, "row", [(row_of(*p), row_of(1 - p[0], *p[1:])) for p in PLACES])


def send_core(v):
    return lax.ppermute(v, "row", [(row_of(*p), row_of(*p[:3], 1 - p[3])) for p in PLACES])


def step(place, along_x, by):
    zh, x, y, core = place
    return row_of(zh, (x + by) % X, y, core) if along_x else row_of(zh, x, (y + by) % Y, core)


def send_small(v, by):
    return lax.ppermute(v, "row", [(row_of(*p), step(p, p[3] == 1, by)) for p in PLACES])


def send_big(v, by):
    return lax.ppermute(v, "row", [(row_of(*p), step(p, p[3] == 0, by)) for p in PLACES])


def send_col(v, by):
    return lax.ppermute(v, "col", [(i, (i + by) % COL) for i in range(COL)])


def gather_over_col(v):
    me = lax.axis_index("col")
    rows = v.shape[0]
    got = [send_col(v, d) for d in (1, 2, 3)]
    every = lax.dynamic_update_slice_in_dim(jnp.zeros((COL * rows, v.shape[1]), v.dtype), v, me * rows, 0)
    for d, block in zip((1, 2, 3), got):
        every = lax.dynamic_update_slice_in_dim(every, block, lax.rem(me + COL - d, COL) * rows, 0)
    return every, got[0]


def sum_along(blocks, send):
    kept = blocks[0]
    for d in (1, 2, 3):
        kept = kept + send(blocks[d].astype(jnp.bfloat16), -d).astype(jnp.float32)
    return kept


def after(v, *earlier):
    return lax.optimization_barrier((v,) + earlier)[0]


def expand(mask):
    rows = mask.shape[0]
    cols = mask.shape[1]
    wide = jnp.broadcast_to(mask[:, None, :, None], (rows, BLOCK, cols, BLOCK))
    return wide.reshape(rows * BLOCK, cols * BLOCK).astype(jnp.bfloat16)


def prune_kernel(gate_mask, up_mask, down_mask, gate, up, down, both_eff, down_eff):
    width = gate.shape[1]
    for mask, source, target, offset in (
        (gate_mask, gate, both_eff, 0),
        (up_mask, up, both_eff, width),
        (down_mask, down, down_eff, 0),
    ):
        for i in range(mask.shape[0]):
            for j in range(mask.shape[1]):
                rows = slice(i * BLOCK, (i + 1) * BLOCK)
                block = source[rows, j * BLOCK : (j + 1) * BLOCK]
                target[rows, offset + j * BLOCK : offset + (j + 1) * BLOCK] = jnp.where(
                    mask[i, j] != 0, block, jnp.zeros_like(block)
                )


def prune(gate_mask, up_mask, down_mask, gate, up, down):
    depth, width = gate.shape
    scalars = pl.BlockSpec(memory_space=pltpu.SMEM)
    whole = pl.BlockSpec(memory_space=pltpu.VMEM)
    return pl.pallas_call(
        prune_kernel,
        in_specs=[scalars] * 3 + [whole] * 3,
        out_specs=[whole] * 2,
        out_shape=[
            jax.ShapeDtypeStruct((depth, 2 * width), jnp.bfloat16),
            jax.ShapeDtypeStruct((width, depth), jnp.bfloat16),
        ],
        compiler_params=pltpu.CompilerParams(vmem_limit_bytes=32 * 1024 * 1024),
    )(gate_mask, up_mask, down_mask, gate, up, down)


def code(part):
    largest = jnp.max(jnp.abs(part), axis=0, keepdims=True)
    power = jnp.clip(jnp.ceil(jnp.log2(largest)), -100.0, 100.0)
    return (part * jnp.exp2(14.0 - power)).astype(jnp.float16), jnp.broadcast_to(power, (8, part.shape[1])).astype(jnp.float16)


def sends_over_col(part, *earlier):
    me = lax.axis_index("col")
    rows = part.shape[0] // COL
    coded, powers = code(part)
    kept = lax.dynamic_slice_in_dim(part, me * rows, rows, 0)
    sent = [
        jnp.concatenate([lax.dynamic_slice_in_dim(coded, lax.rem(me + d, COL) * rows, rows, 0), powers], axis=0)
        for d in (1, 2, 3)
    ]
    sent = lax.optimization_barrier((*sent, *earlier))[:3]
    return [kept] + [send_col(v, d) for v, d in zip(sent, (1, 2, 3))]


def sum_over_col(blocks):
    total = blocks[0]
    rows = total.shape[0]
    for v in blocks[1:]:
        got = v.astype(jnp.float32)
        total = total + got[:rows] * jnp.exp2(got[rows : rows + 1] - 14.0)
    return total


def swiglu_grads(summed, width):
    hiddens, deltas = [], []
    for core in (0, 1):
        gate = summed[:, 2 * core * width : (2 * core + 1) * width]
        up_val = summed[:, (2 * core + 1) * width : (2 * core + 2) * width]
        hidden_grad = summed[:, (4 + core) * width : (5 + core) * width]
        sig = jax.nn.sigmoid(gate)
        swish = gate * sig
        hiddens.append((swish * up_val).astype(jnp.bfloat16))
        deltas.append((hidden_grad * up_val * sig * (1.0 + gate * (1.0 - sig))).astype(jnp.bfloat16))
        deltas.append((hidden_grad * swish).astype(jnp.bfloat16))
    return jnp.concatenate(hiddens, axis=1), jnp.concatenate(deltas, axis=1)


def per_device(
    tokens, out_grad, gate_weight, up_weight, down_weight, gate_mask, up_mask, down_mask
):
    depth, width = gate_weight.shape
    first = jnp.stack([tokens, out_grad])
    second = send_zh(first)

    v = jnp.concatenate([first, second], axis=1)
    v = jnp.concatenate([v] + [send_small(v, d) for d in (1, 2, 3)], axis=1)
    masks = lax.optimization_barrier((gate_mask, up_mask, down_mask, v))[:3]
    both_eff, down_eff = prune(*masks, gate_weight, up_weight, down_weight)
    both_eff = both_eff, send_core(both_eff)
    down_eff = down_eff, send_core(down_eff)

    def forward(own, *earlier):
        parts = [jnp.dot(own[0], w, preferred_element_type=jnp.float32) for w in both_eff]
        parts += [lax.dot_general(own[1], w, TRANSPOSED, preferred_element_type=jnp.float32) for w in down_eff]
        return sends_over_col(jnp.concatenate(parts, axis=1), *earlier)

    def backward(every):
        return sum(
            lax.dot_general(
                every[:, 2 * i * width : 2 * (i + 1) * width], w, TRANSPOSED, preferred_element_type=jnp.float32
            )
            for i, w in enumerate(both_eff)
        )

    near, back, far = send_big(v, 1), send_big(v, 3), send_big(v, 2)
    keeps = [expand(mask) for mask in lax.optimization_barrier((gate_mask, up_mask, down_mask, v))[:3]]
    hidden_a, deltas_a = swiglu_grads(sum_over_col(forward(v)), width)
    near, back, deltas_a, *keeps = lax.optimization_barrier((near, back, deltas_a, *keeps))
    gate_keep, up_keep, down_keep = keeps
    own_b = jnp.concatenate([near, back], axis=1)
    every_a, early_a = gather_over_col(deltas_a)
    hidden_b, deltas_b = swiglu_grads(sum_over_col(forward(own_b, early_a)), width)
    far, deltas_b = lax.optimization_barrier((far, deltas_b))
    every_b, early_b = gather_over_col(deltas_b)
    hidden_c, deltas_c = swiglu_grads(sum_over_col(forward(far, early_b)), width)
    own = jnp.concatenate([v, own_b, far], axis=1)
    other = send_core(own)
    deltas_c, other = lax.optimization_barrier((deltas_c, other))
    every_c, _ = gather_over_col(deltas_c)
    total_a, total_b, total_c = backward(every_a), backward(every_b), backward(every_c)
    rows = total_a.shape[0]
    blocks = total_b[:rows], total_c, total_b[rows:]
    came = [send_big(v.astype(jnp.bfloat16), -d) for v, d in zip(blocks, (1, 2, 3))]
    every = jnp.concatenate([every_a, every_b, every_c], axis=0)
    swapped = send_core(every[:, 2 * width :])
    hiddens = lax.optimization_barrier((hidden_a, hidden_b, hidden_c, swapped))[:3]
    hidden, _ = gather_over_col(jnp.concatenate(hiddens, axis=0))
    hidden = hidden.reshape(COL, -1, 2 * width)
    cuts = jnp.split(hidden, (hidden_a.shape[0], hidden_a.shape[0] + hidden_b.shape[0]), axis=1)
    hidden = jnp.concatenate([cut.reshape(-1, 2 * width) for cut in cuts], axis=0)
    hidden_other = send_core(hidden[:, width:])

    def contract(a, b):
        return lax.dot_general(a, b, CONTRACT, preferred_element_type=jnp.float32)

    gate_grad = contract(own[0], every[:, :width]) + contract(other[0], swapped[:, :width])
    up_grad = contract(own[0], every[:, width : 2 * width]) + contract(other[0], swapped[:, width:])
    gate_grad = gate_grad * gate_keep.astype(jnp.float32)
    up_grad = up_grad * up_keep.astype(jnp.float32)
    total = total_a + came[0].astype(jnp.float32) + came[1].astype(jnp.float32) + came[2].astype(jnp.float32)
    total, gate_grad = lax.optimization_barrier((total, gate_grad))
    blocks = jnp.split(total, 4, axis=0)
    came = [send_small(v.astype(jnp.bfloat16), -d) for v, d in zip(blocks[1:], (1, 2, 3))]
    *came, up_grad = lax.optimization_barrier((*came, up_grad))
    total = blocks[0] + came[0].astype(jnp.float32) + came[1].astype(jnp.float32) + came[2].astype(jnp.float32)
    rows = total.shape[0] // 2
    away = send_zh(total[rows:])
    down_grad = contract(hidden[:, :width], own[1]) + contract(hidden_other, other[1])
    away, down_grad = lax.optimization_barrier((away, down_grad * down_keep.astype(jnp.float32)))
    return total[:rows] + away, gate_grad, up_grad, down_grad


def solution(mesh):
    return jax.shard_map(
        per_device,
        mesh=mesh,
        in_specs=(
            P("row", "col"),
            P("row", "col"),
            P("col", "row"),
            P("col", "row"),
            P("row", "col"),
            P("col", "row"),
            P("col", "row"),
            P("row", "col"),
        ),
        out_specs=(P("row", "col"), P("col", "row"), P("col", "row"), P("row", "col")),
        check_vma=False,
    )
```

```python
import jax
import jax.numpy as jnp
from jax import lax
from jax.experimental import pallas as pl
from jax.experimental.pallas import tpu as pltpu
from jax.sharding import PartitionSpec as P

BLOCK = 128
ZH, X, Y, CORE = 2, 4, 4, 2
COL = 4
TRANSPOSED = (((1,), (1,)), ((), ()))
CONTRACT = (((0,), (0,)), ((), ()))


def row_of(zh, x, y, core):
    return ((zh * X + x) * Y + y) * CORE + core


PLACES = [(zh, x, y, core) for zh in range(ZH) for x in range(X) for y in range(Y) for core in range(CORE)]
def send_zh(v):
    return lax.ppermute(v, "row", [(row_of(*p), row_of(1 - p[0], *p[1:])) for p in PLACES])


def send_core(v):
    return lax.ppermute(v, "row", [(row_of(*p), row_of(*p[:3], 1 - p[3])) for p in PLACES])


def step(place, along_x, by):
    zh, x, y, core = place
    return row_of(zh, (x + by) % X, y, core) if along_x else row_of(zh, x, (y + by) % Y, core)


def send_small(v, by):
    return lax.ppermute(v, "row", [(row_of(*p), step(p, p[3] == 1, by)) for p in PLACES])


def send_big(v, by):
    return lax.ppermute(v, "row", [(row_of(*p), step(p, p[3] == 0, by)) for p in PLACES])


def send_col(v, by):
    return lax.ppermute(v, "col", [(i, (i + by) % COL) for i in range(COL)])


def gather_over_col(v):
    me = lax.axis_index("col")
    rows = v.shape[0]
    got = [send_col(v, d) for d in (1, 2, 3)]
    every = lax.dynamic_update_slice_in_dim(jnp.zeros((COL * rows, v.shape[1]), v.dtype), v, me * rows, 0)
    for d, block in zip((1, 2, 3), got):
        every = lax.dynamic_update_slice_in_dim(every, block, lax.rem(me + COL - d, COL) * rows, 0)
    return every, got[0]


def sum_along(blocks, send):
    kept = blocks[0]
    for d in (1, 2, 3):
        kept = kept + send(blocks[d].astype(jnp.bfloat16), -d).astype(jnp.float32)
    return kept


def after(v, *earlier):
    return lax.optimization_barrier((v,) + earlier)[0]


def expand(mask):
    rows = mask.shape[0]
    cols = mask.shape[1]
    wide = jnp.broadcast_to(mask[:, None, :, None], (rows, BLOCK, cols, BLOCK))
    return wide.reshape(rows * BLOCK, cols * BLOCK).astype(jnp.bfloat16)


def prune_kernel(gate_mask, up_mask, down_mask, gate, up, down, both_eff, down_eff):
    step = pl.program_id(0)
    many = gate.shape[0] // BLOCK

    def keep(scalar, block):
        return jnp.where(scalar != 0, block, jnp.zeros_like(block))

    for mask, source, offset in ((gate_mask, gate, 0), (up_mask, up, gate.shape[1])):
        for i in range(many):
            for j in range(gate.shape[1] // BLOCK):
                rows, cols = slice(i * BLOCK, (i + 1) * BLOCK), j * BLOCK
                block = keep(mask[j, step * many + i], source[rows, cols : cols + BLOCK])
                both_eff[rows, offset + cols : offset + cols + BLOCK] = block
    for i in range(down.shape[0] // BLOCK):
        for j in range(many):
            at = slice(i * BLOCK, (i + 1) * BLOCK), slice(j * BLOCK, (j + 1) * BLOCK)
            down_eff[at] = keep(down_mask[i, step * many + j], down[at])


def prune(gate_mask, up_mask, down_mask, gate, up, down):
    depth, width = gate.shape
    steps = 4
    part = depth // steps
    scalars = pl.BlockSpec(memory_space=pltpu.SMEM)
    return pl.pallas_call(
        prune_kernel,
        grid=(steps,),
        in_specs=[scalars] * 3
        + [pl.BlockSpec((part, width), lambda i: (i, 0))] * 2
        + [pl.BlockSpec((width, part), lambda i: (0, i))],
        out_specs=[
            pl.BlockSpec((part, 2 * width), lambda i: (i, 0)),
            pl.BlockSpec((width, part), lambda i: (0, i)),
        ],
        out_shape=[
            jax.ShapeDtypeStruct((depth, 2 * width), jnp.bfloat16),
            jax.ShapeDtypeStruct((width, depth), jnp.bfloat16),
        ],
        compiler_params=pltpu.CompilerParams(vmem_limit_bytes=32 * 1024 * 1024),
    )(gate_mask.T, up_mask.T, down_mask, gate, up, down)


def code(part):
    largest = jnp.max(jnp.abs(part), axis=0, keepdims=True)
    power = jnp.clip(jnp.ceil(jnp.log2(largest)), -100.0, 100.0)
    return (part * jnp.exp2(14.0 - power)).astype(jnp.float16), jnp.broadcast_to(power, (8, part.shape[1])).astype(jnp.float16)


def sends_over_col(part, *earlier):
    me = lax.axis_index("col")
    rows = part.shape[0] // COL
    coded, powers = code(part)
    kept = lax.dynamic_slice_in_dim(part, me * rows, rows, 0)
    sent = [
        jnp.concatenate([lax.dynamic_slice_in_dim(coded, lax.rem(me + d, COL) * rows, rows, 0), powers], axis=0)
        for d in (1, 2, 3)
    ]
    sent = lax.optimization_barrier((*sent, *earlier))[:3]
    return [kept] + [send_col(v, d) for v, d in zip(sent, (1, 2, 3))]


def sum_over_col(blocks):
    total = blocks[0]
    rows = total.shape[0]
    for v in blocks[1:]:
        got = v.astype(jnp.float32)
        total = total + got[:rows] * jnp.exp2(got[rows : rows + 1] - 14.0)
    return total


def swiglu_grads(summed, width):
    hiddens, deltas = [], []
    for core in (0, 1):
        gate = summed[:, 2 * core * width : (2 * core + 1) * width]
        up_val = summed[:, (2 * core + 1) * width : (2 * core + 2) * width]
        hidden_grad = summed[:, (4 + core) * width : (5 + core) * width]
        sig = jax.nn.sigmoid(gate)
        swish = gate * sig
        hiddens.append((swish * up_val).astype(jnp.bfloat16))
        deltas.append((hidden_grad * up_val * sig * (1.0 + gate * (1.0 - sig))).astype(jnp.bfloat16))
        deltas.append((hidden_grad * swish).astype(jnp.bfloat16))
    return jnp.concatenate(hiddens, axis=1), jnp.concatenate(deltas, axis=1)


def per_device(
    tokens, out_grad, gate_weight, up_weight, down_weight, gate_mask, up_mask, down_mask
):
    depth, width = gate_weight.shape
    first = jnp.stack([tokens, out_grad])
    second = send_zh(first)

    v = jnp.concatenate([first, second], axis=1)
    v = jnp.concatenate([v] + [send_small(v, d) for d in (1, 2, 3)], axis=1)
    both_eff, down_eff = prune(gate_mask, up_mask, down_mask, gate_weight, up_weight, down_weight)
    both_eff = both_eff, send_core(both_eff)
    down_eff = down_eff, send_core(down_eff)

    def forward(own, *earlier):
        parts = [jnp.dot(own[0], w, preferred_element_type=jnp.float32) for w in both_eff]
        parts += [lax.dot_general(own[1], w, TRANSPOSED, preferred_element_type=jnp.float32) for w in down_eff]
        return sends_over_col(jnp.concatenate(parts, axis=1), *earlier)

    def backward(every):
        return sum(
            lax.dot_general(
                every[:, 2 * i * width : 2 * (i + 1) * width], w, TRANSPOSED, preferred_element_type=jnp.float32
            )
            for i, w in enumerate(both_eff)
        )

    near, back, far = send_big(v, 1), send_big(v, 3), send_big(v, 2)
    keeps = [expand(mask) for mask in lax.optimization_barrier((gate_mask, up_mask, down_mask, v))[:3]]
    blocks_a = forward(v)
    near, back, *rest = lax.optimization_barrier((near, back, *keeps, *blocks_a[1:]))
    gate_keep, up_keep, down_keep = rest[:3]
    hidden_a, deltas_a = swiglu_grads(sum_over_col(blocks_a[:1] + rest[3:]), width)
    own_b = jnp.concatenate([near, back], axis=1)
    every_a, early_a = gather_over_col(deltas_a)
    blocks_b = forward(own_b, early_a)
    far, *rest = lax.optimization_barrier((far, *blocks_b[1:]))
    hidden_b, deltas_b = swiglu_grads(sum_over_col(blocks_b[:1] + rest), width)
    every_b, early_b = gather_over_col(deltas_b)
    hidden_c, deltas_c = swiglu_grads(sum_over_col(forward(far, early_b)), width)
    own = jnp.concatenate([v, own_b, far], axis=1)
    other = send_core(own)
    deltas_c, other = lax.optimization_barrier((deltas_c, other))
    every_c, _ = gather_over_col(deltas_c)
    total_a, total_b, total_c = backward(every_a), backward(every_b), backward(every_c)
    rows = total_a.shape[0]
    blocks = total_b[:rows], total_c, total_b[rows:]
    came = [send_big(v.astype(jnp.bfloat16), -d) for v, d in zip(blocks, (1, 2, 3))]
    every = jnp.concatenate([every_a, every_b, every_c], axis=0)
    swapped = send_core(every[:, 2 * width :])
    hiddens = lax.optimization_barrier((hidden_a, hidden_b, hidden_c, swapped))[:3]
    hidden, _ = gather_over_col(jnp.concatenate(hiddens, axis=0))
    hidden = hidden.reshape(COL, -1, 2 * width)
    cuts = jnp.split(hidden, (hidden_a.shape[0], hidden_a.shape[0] + hidden_b.shape[0]), axis=1)
    hidden = jnp.concatenate([cut.reshape(-1, 2 * width) for cut in cuts], axis=0)
    hidden_other = send_core(hidden[:, width:])

    def contract(a, b):
        return lax.dot_general(a, b, CONTRACT, preferred_element_type=jnp.float32)

    gate_grad = contract(own[0], every[:, :width]) + contract(other[0], swapped[:, :width])
    up_grad = contract(own[0], every[:, width : 2 * width]) + contract(other[0], swapped[:, width:])
    gate_grad = gate_grad * gate_keep.astype(jnp.float32)
    up_grad = up_grad * up_keep.astype(jnp.float32)
    total = total_a + came[0].astype(jnp.float32) + came[1].astype(jnp.float32) + came[2].astype(jnp.float32)
    total, gate_grad = lax.optimization_barrier((total, gate_grad))
    blocks = jnp.split(total, 4, axis=0)
    came = [send_small(v.astype(jnp.bfloat16), -d) for v, d in zip(blocks[1:], (1, 2, 3))]
    *came, up_grad = lax.optimization_barrier((*came, up_grad))
    total = blocks[0] + came[0].astype(jnp.float32) + came[1].astype(jnp.float32) + came[2].astype(jnp.float32)
    rows = total.shape[0] // 2
    away = send_zh(total[rows:])
    down_grad = contract(hidden[:, :width], own[1]) + contract(hidden_other, other[1])
    away, down_grad = lax.optimization_barrier((away, down_grad * down_keep.astype(jnp.float32)))
    return total[:rows] + away, gate_grad, up_grad, down_grad


def solution(mesh):
    return jax.shard_map(
        per_device,
        mesh=mesh,
        in_specs=(
            P("row", "col"),
            P("row", "col"),
            P("col", "row"),
            P("col", "row"),
            P("row", "col"),
            P("col", "row"),
            P("col", "row"),
            P("row", "col"),
        ),
        out_specs=(P("row", "col"), P("col", "row"), P("col", "row"), P("row", "col")),
        check_vma=False,
    )
```

```python
import jax
import jax.numpy as jnp
from jax import lax
from jax.experimental import pallas as pl
from jax.experimental.pallas import tpu as pltpu
from jax.sharding import PartitionSpec as P

BLOCK = 128
ZH, X, Y, CORE = 2, 4, 4, 2
COL = 4
TRANSPOSED = (((1,), (1,)), ((), ()))
CONTRACT = (((0,), (0,)), ((), ()))


def row_of(zh, x, y, core):
    return ((zh * X + x) * Y + y) * CORE + core


PLACES = [(zh, x, y, core) for zh in range(ZH) for x in range(X) for y in range(Y) for core in range(CORE)]
def send_zh(v):
    return lax.ppermute(v, "row", [(row_of(*p), row_of(1 - p[0], *p[1:])) for p in PLACES])


def send_core(v):
    return lax.ppermute(v, "row", [(row_of(*p), row_of(*p[:3], 1 - p[3])) for p in PLACES])


def step(place, along_x, by):
    zh, x, y, core = place
    return row_of(zh, (x + by) % X, y, core) if along_x else row_of(zh, x, (y + by) % Y, core)


def send_small(v, by):
    return lax.ppermute(v, "row", [(row_of(*p), step(p, p[3] == 1, by)) for p in PLACES])


def send_big(v, by):
    return lax.ppermute(v, "row", [(row_of(*p), step(p, p[3] == 0, by)) for p in PLACES])


def send_col(v, by):
    return lax.ppermute(v, "col", [(i, (i + by) % COL) for i in range(COL)])


def gather_over_col(v):
    me = lax.axis_index("col")
    rows = v.shape[0]
    got = [send_col(v, d) for d in (1, 2, 3)]
    every = lax.dynamic_update_slice_in_dim(jnp.zeros((COL * rows, v.shape[1]), v.dtype), v, me * rows, 0)
    for d, block in zip((1, 2, 3), got):
        every = lax.dynamic_update_slice_in_dim(every, block, lax.rem(me + COL - d, COL) * rows, 0)
    return every, got[0]


def sum_along(blocks, send):
    kept = blocks[0]
    for d in (1, 2, 3):
        kept = kept + send(blocks[d].astype(jnp.bfloat16), -d).astype(jnp.float32)
    return kept


def after(v, *earlier):
    return lax.optimization_barrier((v,) + earlier)[0]


def expand(mask):
    rows = mask.shape[0]
    cols = mask.shape[1]
    wide = jnp.broadcast_to(mask[:, None, :, None], (rows, BLOCK, cols, BLOCK))
    return wide.reshape(rows * BLOCK, cols * BLOCK).astype(jnp.bfloat16)


def prune_kernel(gate_mask, up_mask, down_mask, gate, up, down, both_eff, down_eff):
    step = pl.program_id(0)
    many = gate.shape[0] // BLOCK

    def keep(scalar, block):
        return jnp.where(scalar != 0, block, jnp.zeros_like(block))

    for mask, source, offset in ((gate_mask, gate, 0), (up_mask, up, gate.shape[1])):
        for i in range(many):
            for j in range(gate.shape[1] // BLOCK):
                rows, cols = slice(i * BLOCK, (i + 1) * BLOCK), j * BLOCK
                block = keep(mask[j, step * many + i], source[rows, cols : cols + BLOCK])
                both_eff[rows, offset + cols : offset + cols + BLOCK] = block
    for i in range(down.shape[0] // BLOCK):
        for j in range(many):
            at = slice(i * BLOCK, (i + 1) * BLOCK), slice(j * BLOCK, (j + 1) * BLOCK)
            down_eff[at] = keep(down_mask[i, step * many + j], down[at])


def prune(gate_mask, up_mask, down_mask, gate, up, down):
    depth, width = gate.shape
    steps = 4
    part = depth // steps
    scalars = pl.BlockSpec(memory_space=pltpu.SMEM)
    return pl.pallas_call(
        prune_kernel,
        grid=(steps,),
        in_specs=[scalars] * 3
        + [pl.BlockSpec((part, width), lambda i: (i, 0))] * 2
        + [pl.BlockSpec((width, part), lambda i: (0, i))],
        out_specs=[
            pl.BlockSpec((part, 2 * width), lambda i: (i, 0)),
            pl.BlockSpec((width, part), lambda i: (0, i)),
        ],
        out_shape=[
            jax.ShapeDtypeStruct((depth, 2 * width), jnp.bfloat16),
            jax.ShapeDtypeStruct((width, depth), jnp.bfloat16),
        ],
        compiler_params=pltpu.CompilerParams(vmem_limit_bytes=60 * 1024 * 1024),
    )(gate_mask.T, up_mask.T, down_mask, gate, up, down)


def code(part):
    largest = jnp.max(jnp.abs(part), axis=0, keepdims=True)
    power = jnp.clip(jnp.ceil(jnp.log2(largest)), -100.0, 100.0)
    return (part * jnp.exp2(14.0 - power)).astype(jnp.float16), jnp.broadcast_to(power, (8, part.shape[1])).astype(jnp.float16)


def sends_over_col(part, *earlier):
    me = lax.axis_index("col")
    rows = part.shape[0] // COL
    coded, powers = code(part)
    kept = lax.dynamic_slice_in_dim(part, me * rows, rows, 0)
    sent = [
        jnp.concatenate([lax.dynamic_slice_in_dim(coded, lax.rem(me + d, COL) * rows, rows, 0), powers], axis=0)
        for d in (1, 2, 3)
    ]
    sent = lax.optimization_barrier((*sent, *earlier))[:3]
    return [kept] + [send_col(v, d) for v, d in zip(sent, (1, 2, 3))]


def sum_over_col(blocks):
    total = blocks[0]
    rows = total.shape[0]
    for v in blocks[1:]:
        got = v.astype(jnp.float32)
        total = total + got[:rows] * jnp.exp2(got[rows : rows + 1] - 14.0)
    return total


def swiglu_grads(summed, width):
    hiddens, deltas = [], []
    for core in (0, 1):
        gate = summed[:, 2 * core * width : (2 * core + 1) * width]
        up_val = summed[:, (2 * core + 1) * width : (2 * core + 2) * width]
        hidden_grad = summed[:, (4 + core) * width : (5 + core) * width]
        sig = jax.nn.sigmoid(gate)
        swish = gate * sig
        hiddens.append((swish * up_val).astype(jnp.bfloat16))
        deltas.append((hidden_grad * up_val * sig * (1.0 + gate * (1.0 - sig))).astype(jnp.bfloat16))
        deltas.append((hidden_grad * swish).astype(jnp.bfloat16))
    return jnp.concatenate(hiddens, axis=1), jnp.concatenate(deltas, axis=1)


def per_device(
    tokens, out_grad, gate_weight, up_weight, down_weight, gate_mask, up_mask, down_mask
):
    depth, width = gate_weight.shape
    first = jnp.stack([tokens, out_grad])
    second = send_zh(first)

    v = jnp.concatenate([first, second], axis=1)
    v = jnp.concatenate([v] + [send_small(v, d) for d in (1, 2, 3)], axis=1)
    both_eff, down_eff = prune(gate_mask, up_mask, down_mask, gate_weight, up_weight, down_weight)
    both_eff = both_eff, send_core(both_eff)
    down_eff = down_eff, send_core(down_eff)

    def forward(own, *earlier):
        parts = [jnp.dot(own[0], w, preferred_element_type=jnp.float32) for w in both_eff]
        parts += [lax.dot_general(own[1], w, TRANSPOSED, preferred_element_type=jnp.float32) for w in down_eff]
        return sends_over_col(jnp.concatenate(parts, axis=1), *earlier)

    def backward(every):
        return sum(
            lax.dot_general(
                every[:, 2 * i * width : 2 * (i + 1) * width], w, TRANSPOSED, preferred_element_type=jnp.float32
            )
            for i, w in enumerate(both_eff)
        )

    near, back, far = send_big(v, 1), send_big(v, 3), send_big(v, 2)
    keeps = [expand(mask) for mask in lax.optimization_barrier((gate_mask, up_mask, down_mask, v))[:3]]
    blocks_a = forward(v)
    near, back, *rest = lax.optimization_barrier((near, back, *keeps, *blocks_a[1:]))
    gate_keep, up_keep, down_keep = rest[:3]
    hidden_a, deltas_a = swiglu_grads(sum_over_col(blocks_a[:1] + rest[3:]), width)
    own_b = jnp.concatenate([near, back], axis=1)
    every_a, early_a = gather_over_col(deltas_a)
    blocks_b = forward(own_b, early_a)
    far, *rest = lax.optimization_barrier((far, *blocks_b[1:]))
    hidden_b, deltas_b = swiglu_grads(sum_over_col(blocks_b[:1] + rest), width)
    every_b, early_b = gather_over_col(deltas_b)
    hidden_c, deltas_c = swiglu_grads(sum_over_col(forward(far, early_b)), width)
    own = jnp.concatenate([v, own_b, far], axis=1)
    other = send_core(own)
    deltas_c, other = lax.optimization_barrier((deltas_c, other))
    every_c, _ = gather_over_col(deltas_c)
    total_a, total_b, total_c = backward(every_a), backward(every_b), backward(every_c)
    rows = total_a.shape[0]
    blocks = total_b[:rows], total_c, total_b[rows:]
    came = [send_big(v.astype(jnp.bfloat16), -d) for v, d in zip(blocks, (1, 2, 3))]
    every = jnp.concatenate([every_a, every_b, every_c], axis=0)
    swapped = send_core(every[:, 2 * width :])
    hiddens = lax.optimization_barrier((hidden_a, hidden_b, hidden_c, swapped))[:3]
    hidden, _ = gather_over_col(jnp.concatenate(hiddens, axis=0))
    hidden = hidden.reshape(COL, -1, 2 * width)
    cuts = jnp.split(hidden, (hidden_a.shape[0], hidden_a.shape[0] + hidden_b.shape[0]), axis=1)
    hidden = jnp.concatenate([cut.reshape(-1, 2 * width) for cut in cuts], axis=0)
    hidden_other = send_core(hidden[:, width:])

    def contract(a, b):
        return lax.dot_general(a, b, CONTRACT, preferred_element_type=jnp.float32)

    gate_grad = contract(own[0], every[:, :width]) + contract(other[0], swapped[:, :width])
    up_grad = contract(own[0], every[:, width : 2 * width]) + contract(other[0], swapped[:, width:])
    gate_grad = gate_grad * gate_keep.astype(jnp.float32)
    up_grad = up_grad * up_keep.astype(jnp.float32)
    total = total_a + came[0].astype(jnp.float32) + came[1].astype(jnp.float32) + came[2].astype(jnp.float32)
    total, gate_grad = lax.optimization_barrier((total, gate_grad))
    blocks = jnp.split(total, 4, axis=0)
    came = [send_small(v.astype(jnp.bfloat16), -d) for v, d in zip(blocks[1:], (1, 2, 3))]
    *came, up_grad = lax.optimization_barrier((*came, up_grad))
    total = blocks[0] + came[0].astype(jnp.float32) + came[1].astype(jnp.float32) + came[2].astype(jnp.float32)
    rows = total.shape[0] // 2
    away = send_zh(total[rows:])
    down_grad = contract(hidden[:, :width], own[1]) + contract(hidden_other, other[1])
    away, down_grad = lax.optimization_barrier((away, down_grad * down_keep.astype(jnp.float32)))
    return total[:rows] + away, gate_grad, up_grad, down_grad


def solution(mesh):
    return jax.shard_map(
        per_device,
        mesh=mesh,
        in_specs=(
            P("row", "col"),
            P("row", "col"),
            P("col", "row"),
            P("col", "row"),
            P("row", "col"),
            P("col", "row"),
            P("col", "row"),
            P("row", "col"),
        ),
        out_specs=(P("row", "col"), P("col", "row"), P("col", "row"), P("row", "col")),
        check_vma=False,
    )
```
